128 devices in a mesh: grp: 8 (over x_hi, y), gx: 16 (over x_lo, z, core).
Axes of the slice: x: 4 (x_hi: 2, x_lo: 2; x = x_hi * 2 + x_lo), y: 4, z: 4, core: 2. Of those that a mesh axis runs over, the one named last changes fastest.
Arguments:
- velocity: float32 [3, 128, 128, 4096], P(None, 'grp', 'gx'), may hold values from -6 to 6
- noise: float32 [3, 8, 128, 4096], P(None, None, None, 'gx'), may hold values from -6 to 6
- previous: float32 [3, 128, 4096], P(None, None, 'gx'), may hold values from -6 to 6
- decay: float32 [3, 128], replicated, may hold values from 0.6 to 0.99
- stress_factor: float32 [6, 128], replicated, may hold values from 0.2 to 1
- mean_profile: float32 [128], replicated, may hold values from 0.5 to 1.5
Outputs:
- advanced_velocity: float32 [3, 128, 128, 4096], P(None, 'grp', 'gx')
The draws below stay inside these ranges and needn't reach their ends.
All inputs are finite; a program needn't handle non-finite values.
Results may differ from the reference program's by a relative error of at most 0.0003.
Values sent between devices are 32-bit elements; how exact they have to be, the bound alone decides.
A program may use at most 128 MiB of HBM per device.

```python
import math
import jax
import jax.numpy as jnp

HALF = 32
PL = 8
NY = 4096
NX = 128
NZ = 128


def draw_noise(key, part):
    keys = jax.random.split(key, 5)
    shape = (3, PL, NZ, NY)
    base = jax.random.normal(keys[0], shape, jnp.float32)
    amp_span = jax.random.uniform(keys[1], (3, 1, 1, 1), jnp.float32, 1.5, 2.5)
    amp_wall = jax.random.uniform(keys[2], (3, 1, 1, 1), jnp.float32, 1.5, 2.5)
    phase_span = jax.random.uniform(keys[3], (3, 1, 1, 1), jnp.float32, 0.0, 2.0 * math.pi)
    phase_wall = jax.random.uniform(keys[4], (3, 1, 1, 1), jnp.float32, 0.0, 2.0 * math.pi)
    z_index = jnp.arange(NZ)
    y_index = jnp.arange(NY)
    z_pos = z_index.astype(jnp.float32)[None, None, :, None]
    y_pos = y_index.astype(jnp.float32)[None, None, None, :]
    z_sign = (1 - 2 * (z_index % 2)).astype(jnp.float32)[None, None, :, None]
    y_sign = (1 - 2 * (y_index % 2)).astype(jnp.float32)[None, None, None, :]
    smooth_z = amp_span * (1.0 + 0.4 * jnp.cos(2.0 * math.pi * z_pos / NZ + phase_span))
    smooth_y = amp_wall * (1.0 + 0.4 * jnp.cos(2.0 * math.pi * y_pos / NY + phase_wall))
    total = base + y_sign * smooth_z + z_sign * smooth_y
    return jnp.clip(total, -6.0, 6.0).astype(jnp.float32)


def steps_of(own_key, extent, cuts, smallest, high):
    factor_of, own = 1.0, jax.random.fold_in(own_key, 6)
    for dim, shards_of in cuts:
        draws = jnp.exp(jax.random.uniform(jax.random.fold_in(own, dim), (shards_of,), jnp.float32, smallest / len(cuts), high / len(cuts)))
        factor_of = factor_of * jnp.repeat(draws, extent[dim] // shards_of).reshape([-1 if axis == dim else 1 for axis in range(len(extent))])
    return factor_of


def scatter_about(stream_key, shape, scale, bound, cuts=(), kind=jnp.bfloat16):
    level = steps_of(stream_key, shape, cuts, -0.22, 0.18) if cuts else 1.0
    values = jax.random.normal(stream_key, shape, jnp.float32) * scale * level
    return jnp.minimum(jnp.maximum(values, -bound), bound).astype(kind)


def setup_inputs(seed: int = 0) -> dict:
    arg_keys = jax.random.split(jax.random.key(seed), 7)
    velocity = scatter_about(arg_keys[0], (3, NX, NZ, NY), 1.0, 6.0, ((1, 8), (2, 16)), jnp.float32)
    noise = draw_noise(jax.random.fold_in(arg_keys[6], 71), 0)
    previous = scatter_about(arg_keys[2], (3, NZ, NY), 1.0, 6.0, ((2, 16),), jnp.float32)
    decay = jnp.clip(jnp.exp(jax.random.uniform(arg_keys[3], (3, NZ), jnp.float32, math.log(0.6), math.log(0.99))), 0.6, 0.99)
    stress_factor = jnp.clip(jax.random.uniform(arg_keys[4], (6, NZ), jnp.float32, 0.2, 1.0), 0.2, 1.0)
    mean_profile = jnp.clip(jax.random.uniform(arg_keys[5], (NZ,), jnp.float32, 0.5, 1.5), 0.5, 1.5)
    return {"velocity": velocity, "noise": noise, "previous": previous, "decay": decay, "stress_factor": stress_factor, "mean_profile": mean_profile}


TIME_STEP = 0.15
VISCOSITY = 0.2

def kernel_weight(offset):
    length = HALF / 2.0
    return jnp.exp(-jnp.pi * offset * offset / (2.0 * length * length))

def kernel_norm():
    offsets = jnp.arange(-HALF, HALF + 1).astype(jnp.float32)
    return jnp.sqrt(jnp.sum(kernel_weight(offsets) ** 2))

def smooth(noise):
    norm = kernel_norm()
    along_y = jnp.zeros_like(noise)
    for offset in range(-HALF, HALF + 1):
        weight = kernel_weight(jnp.float32(offset)) / norm
        along_y = along_y + weight * jnp.roll(noise, -offset, axis=3)
    padded = jnp.pad(along_y, ((0, 0), (0, 0), (HALF, HALF), (0, 0)))
    result = jnp.zeros_like(noise)
    for offset in range(-HALF, HALF + 1):
        weight = kernel_weight(jnp.float32(offset)) / norm
        result = result + weight * padded[:, :, HALF + offset:HALF + offset + NZ]
    return result

def colour(planes, stress_factor, mean_profile):
    factor = stress_factor[:, None, :, None]
    first = mean_profile[None, :, None] + factor[0] * planes[0]
    second = factor[1] * planes[0] + factor[2] * planes[1]
    third = factor[3] * planes[0] + factor[4] * planes[1] + factor[5] * planes[2]
    return jnp.stack([first, second, third])

def tendency(padded):
    centre = padded[:, 1:-1, 1:-1]
    x_next = padded[:, 2:, 1:-1]
    x_prev = padded[:, :-2, 1:-1]
    z_next = padded[:, 1:-1, 2:]
    z_prev = padded[:, 1:-1, :-2]
    y_next = jnp.roll(centre, -1, axis=3)
    y_prev = jnp.roll(centre, 1, axis=3)
    advect = centre[0:1] * (x_next - x_prev) * 0.5
    advect = advect + centre[1:2] * (z_next - z_prev) * 0.5
    advect = advect + centre[2:3] * (y_next - y_prev) * 0.5
    spread = x_next + x_prev + z_next + z_prev + y_next + y_prev - 6.0 * centre
    return -advect + VISCOSITY * spread

def pad_faces(field):
    return jnp.pad(field, ((0, 0), (1, 1), (1, 1), (0, 0)))

def reference(velocity, noise, previous, decay, stress_factor, mean_profile):
    smoothed = smooth(noise)
    decay_col = decay[:, :, None]
    scale_col = jnp.sqrt(1.0 - decay_col * decay_col)
    carried = previous
    outputs = []
    for plane_index in range(PL):
        carried = decay_col * carried + scale_col * smoothed[:, plane_index]
        outputs.append(carried)
    planes = jnp.stack(outputs, axis=1)
    inflow = colour(planes, stress_factor, mean_profile)
    start = velocity.at[:, :PL].set(inflow)
    section = start + TIME_STEP * tendency(pad_faces(start))
    second = section + TIME_STEP * tendency(pad_faces(section))
    return 0.5 * start + 0.5 * second
```

```python
import functools

import jax
import jax.numpy as jnp
import ml_dtypes
import numpy as np
from jax import lax
from jax.experimental import pallas as pl
from jax.experimental.pallas import tpu as pltpu
from jax.sharding import PartitionSpec as P

HALF = 32
TIME_STEP = 0.15
VISCOSITY = 0.2
PL = 8
ROWS, COLS = 8, 16
NX, NZ, NY = 16, 8, 4096
SPAN = NY // COLS
DEPTH = NZ * COLS
WIDE = 512
MESH = pl.DeviceIdType.MESH
F32, BF16 = jnp.float32, jnp.bfloat16

PLANES = {0: (0, 4, 5, 6), 1: (1,), 3: (2,), 4: (3, 7)}
SLOTS = max(len(v) for v in PLANES.values())
OWNER = {p: (r, j) for r, v in PLANES.items() for j, p in enumerate(v)}

GROUPS = ((0, 2), (2, 2), (4, 2), (6, 2), (8, 4), (12, 4))
NG = len(GROUPS)


def weights():
    k = np.arange(-HALF, HALF + 1, dtype=np.float64)
    length = HALF / 2.0
    w = np.exp(-np.pi * k * k / (2.0 * length * length))
    w = w / np.sqrt(np.sum(w * w))

    def band(distance):
        inside = np.abs(distance) <= HALF
        return np.where(inside, w[np.clip(distance + HALF, 0, 2 * HALF)], 0.0)

    cols = np.arange(SPAN)[None, :]
    main = band(np.arange(SPAN)[:, None] - cols)
    wy = np.zeros((3, SPAN + 256, SPAN))
    for c in range(3):
        wy[c, :SPAN] = main
        rim = np.arange(HALF)[:, None]
        wy[c, SPAN + HALF * c : SPAN + HALF * (c + 1)] = band(rim - HALF - cols)
        wy[c, SPAN + 128 + HALF * c : SPAN + 128 + HALF * (c + 1)] = band(rim + SPAN - cols)
    wz = band(np.arange(DEPTH)[:, None] - np.arange(DEPTH)[None, :])

    def split(a):
        a = a.astype(np.float32)
        hi = a.astype(ml_dtypes.bfloat16)
        lo = (a - hi.astype(np.float32)).astype(ml_dtypes.bfloat16)
        return hi, lo

    return split(wy) + split(wz)


def split_bf16(value):
    hi = value.astype(BF16)
    return hi, (value - hi.astype(F32)).astype(BF16)


def dot3(a, b):
    def dot(x, y):
        return jnp.dot(x, y, preferred_element_type=F32)

    return dot(a[0], b[0]) + (dot(a[1], b[0]) + dot(a[0], b[1]))


def kernel(
    vel, noise, prev, decay, stress, mean, wyh, wyl, wzh, wzl, out,
    v, s, o, hz, nz, pv, rim_out, rim_in, sm, mid, infl, psi, cols, dec,
    load_sem, rim_s, rim_r, a_s, a_r, a_l, b_s, b_r, b_l, z_s, z_r, x_s, x_r, out_sem,
):
    r, g = lax.axis_index("grp"), lax.axis_index("gx")
    xl, z, core = g // 8, lax.rem(g // 2, 4), lax.rem(g, 2)

    def by_row(values, default):
        picked = jnp.int32(default)
        for row, value in values.items():
            picked = jnp.where(r == row, value, picked)
        return picked

    count = by_row({row: len(p) for row, p in PLANES.items()}, 0)
    plane_of = [
        by_row({row: (p[j] if j < len(p) else 0) for row, p in PLANES.items()}, 0)
        for j in range(SLOTS)
    ]
    up, down = lax.rem(g + 1, COLS), lax.rem(g + COLS - 1, COLS)

    def remote(src, dst, send, recv, row, col):
        return pltpu.make_async_remote_copy(
            src_ref=src, dst_ref=dst, send_sem=send, recv_sem=recv,
            device_id=(row, col), device_id_type=MESH,
        )

    def each_slot(body):
        for j in range(SLOTS):
            pl.when(j < count)(functools.partial(body, j))

    def noise_load(j):
        return pltpu.make_async_copy(noise.at[:, plane_of[j]], nz.at[j], load_sem.at[j])

    def prev_load():
        return pltpu.make_async_copy(prev, pv, load_sem.at[SLOTS])

    def vel_load(i):
        return pltpu.make_async_copy(
            vel.at[:, pl.ds(8 * i, 8)], v.at[:, pl.ds(1 + 8 * i, 8)], load_sem.at[SLOTS + 1 + i]
        )

    each_slot(lambda j: noise_load(j).start())
    pl.when(r == 0)(lambda: prev_load().start())
    vel_load(1).start()
    pl.when(r != 0)(lambda: vel_load(0).start())

    barrier = pltpu.get_barrier_semaphore()

    def greet(row, col):
        pl.semaphore_signal(barrier, 1, device_id=(row, col), device_id_type=MESH)

    greet(r, up)
    greet(r, down)
    pl.when(r > 0)(lambda: greet(r - 1, g))
    pl.when(r < ROWS - 1)(lambda: greet(r + 1, g))

    @pl.when(count > 0)
    def _():
        for k in (1, 2, 3):
            greet(r, xl * 8 + lax.rem(z + k, 4) * 2 + core)

    @pl.when(r == 0)
    def _():
        for row in PLANES:
            for xs in range(2):
                for cs in range(2):
                    if row == 0:
                        @pl.when(jnp.logical_or(xs != xl, cs != core))
                        def _():
                            greet(row, xs * 8 + z * 2 + cs)
                    else:
                        greet(row, xs * 8 + z * 2 + cs)

    row_i = lax.broadcasted_iota(jnp.int32, (NZ, 128), 0)
    lane_i = lax.broadcasted_iota(jnp.int32, (NZ, 128), 1)

    @pl.when(r == 0)
    def _():
        mine = lane_i == row_i + NZ * g

        def column(row):
            picked = jnp.where(mine, row, 0.0)
            return jnp.broadcast_to(jnp.sum(picked, axis=1, keepdims=True), (NZ, 128))

        for c in range(3):
            cols[c] = column(decay[c : c + 1, :])
        for c in range(6):
            cols[3 + c] = column(stress[c : c + 1, :])
        cols[9] = column(mean[...])

    @pl.when(count > 0)
    def _():
        row_d = lax.broadcasted_iota(jnp.int32, (DEPTH, 128), 0)
        lane_d = lax.broadcasted_iota(jnp.int32, (DEPTH, 128), 1)
        for c in range(3):
            picked = jnp.where(row_d == lane_d, decay[c : c + 1, :], 0.0)
            dec[c] = jnp.broadcast_to(jnp.sum(picked, axis=1, keepdims=True), (DEPTH, 128))

    @pl.when(g == 0)
    def _():
        hz[0, 0] = jnp.zeros(hz.shape[2:], F32)
        hz[1, 0] = jnp.zeros(hz.shape[2:], F32)

    @pl.when(g == COLS - 1)
    def _():
        hz[0, 1] = jnp.zeros(hz.shape[2:], F32)
        hz[1, 1] = jnp.zeros(hz.shape[2:], F32)

    def clear_x(at):
        for c in range(3):
            v[c, at] = jnp.zeros((NZ, NY), F32)
            s[c, at] = jnp.zeros((NZ, NY), F32)

    pl.when(r == 0)(lambda: clear_x(0))
    pl.when(r == ROWS - 1)(lambda: clear_x(NX + 1))

    def pack(j):
        noise_load(j).wait()
        lane = lax.broadcasted_iota(jnp.int32, (DEPTH, 128), 1)
        high = jnp.zeros((DEPTH, 128), F32)
        low = jnp.zeros((DEPTH, 128), F32)
        for c in range(3):
            here = jnp.logical_and(lane >= HALF * c, lane < HALF * (c + 1))
            last = nz[j, c, :, SPAN - 128 :]
            first = nz[j, c, :, :128]
            high = jnp.where(here, pltpu.roll(last, (HALF * c + HALF) % 128, 1), high)
            low = jnp.where(here, pltpu.roll(first, HALF * c, 1) if c else first, low)
        rim_out[j, 0] = high
        rim_out[j, 1] = low

    each_slot(pack)

    waits = 2 + (r > 0).astype(jnp.int32) + (r < ROWS - 1).astype(jnp.int32)
    waits = waits + jnp.where(count > 0, 7, 0) - (r == 0).astype(jnp.int32)
    pl.semaphore_wait(barrier, waits)

    def rims(j):
        return (
            remote(rim_out.at[j, 0], rim_in.at[j, 0], rim_s.at[j, 0], rim_r.at[j, 0], r, up),
            remote(rim_out.at[j, 1], rim_in.at[j, 1], rim_s.at[j, 1], rim_r.at[j, 1], r, down),
        )

    def send_rims(j):
        for copy in rims(j):
            copy.start()

    each_slot(send_rims)

    field = (v, s)

    def z_face(stage, n, side):
        first, width = GROUPS[n]
        row = NZ - 1 if side == 0 else 0
        return remote(
            field[stage].at[:, pl.ds(1 + first, width), row],
            hz.at[stage, side, :, pl.ds(first, width), 0],
            z_s.at[stage, side, n], z_r.at[stage, side, n], r, up if side == 0 else down,
        )

    def send_z(stage, n):
        pl.when(g < COLS - 1)(lambda: z_face(stage, n, 0).start())
        pl.when(g > 0)(lambda: z_face(stage, n, 1).start())

    def recv_z(stage, n):
        pl.when(g > 0)(lambda: z_face(stage, n, 0).wait_recv())
        pl.when(g < COLS - 1)(lambda: z_face(stage, n, 1).wait_recv())

    def sent_z(stage, n):
        pl.when(g < COLS - 1)(lambda: z_face(stage, n, 0).wait_send())
        pl.when(g > 0)(lambda: z_face(stage, n, 1).wait_send())

    def x_face(stage, side):
        src, dst, row = (NX, 0, r + 1) if side == 0 else (1, NX + 1, r - 1)
        return remote(
            field[stage].at[:, src], field[stage].at[:, dst],
            x_s.at[stage, side], x_r.at[stage, side], row, g,
        )

    def send_x(stage, side):
        pl.when(r < ROWS - 1 if side == 0 else r > 0)(lambda: x_face(stage, side).start())

    def sent_x(stage, side):
        pl.when(r < ROWS - 1 if side == 0 else r > 0)(lambda: x_face(stage, side).wait_send())

    def recv_x(stage, side):
        pl.when(r > 0 if side == 0 else r < ROWS - 1)(lambda: x_face(stage, side).wait_recv())

    def a_copy(j, k):
        there = lax.rem(z + k, 4)
        return remote(
            sm.at[j, :, :, there], mid.at[j, z], a_s.at[j, k], a_r.at[j, k],
            r, xl * 8 + there * 2 + core,
        )

    def a_local(j):
        return pltpu.make_async_copy(sm.at[j, :, :, z], mid.at[j, z], a_l.at[j])

    def smooth(j):
        for copy in rims(j):
            copy.wait_recv()
        rim = jnp.concatenate([rim_in[j, 0], rim_in[j, 1]], axis=1)
        rim = split_bf16(rim)

        def one(c, carry):
            main = split_bf16(nz[j, c])
            a = tuple(jnp.concatenate([m, w], axis=1) for m, w in zip(main, rim))
            along_y = dot3(a, (wyh[c], wyl[c]))
            done = dot3((wzh[...], wzl[...]), split_bf16(along_y))
            d = dec[c][:, :1]
            done = jnp.sqrt(1.0 - d * d) * done
            sm[j, c] = done.reshape(2, 4, 2, NZ, SPAN)
            return carry

        lax.fori_loop(0, 3, one, 0)
        if j == 0:
            @pl.when(r == 0)
            def _():
                prev_load().wait()
                for c in range(3):
                    first = sm[j, c].reshape(DEPTH, SPAN) + dec[c][:, :1] * pv[c]
                    sm[j, c] = first.reshape(2, 4, 2, NZ, SPAN)
        for k in (2, 1, 3):
            a_copy(j, k).start()
        a_local(j).start()

    def b_copy(j, p, xd, cd):
        return remote(
            mid.at[j, :, :, xd, cd], infl.at[p, xl, core], b_s.at[j, xd, cd], b_r.at[p, xl, core],
            0, xd * 8 + z * 2 + cd,
        )

    def b_local(j, p):
        return pltpu.make_async_copy(mid.at[j, :, :, xl, core], infl.at[p, xl, core], b_l.at[j])

    def leaving(xd, cd):
        return jnp.logical_or(r != 0, jnp.logical_or(xl != xd, core != cd))

    def forward(j):
        for k in (1, 3, 2):
            a_copy(j, k).wait()
        a_local(j).wait()
        p = plane_of[j]
        for xd in range(2):
            for cd in range(2):
                pl.when(leaving(xd, cd))(lambda: b_copy(j, p, xd, cd).start())
        pl.when(r == 0)(lambda: b_local(j, p).start())

    def forwarded(j):
        p = plane_of[j]
        for xd in range(2):
            for cd in range(2):
                pl.when(leaving(xd, cd))(lambda: b_copy(j, p, xd, cd).wait_send())
        for copy in rims(j):
            copy.wait_send()

    def inflow(p):
        owner, j = OWNER[p]
        for xs in range(2):
            for cs in range(2):
                arrival = remote(
                    mid.at[j, :, :, 0, 0], infl.at[p, xs, cs], b_s.at[0, 0, 0], b_r.at[p, xs, cs],
                    0, xs * 8 + z * 2 + cs,
                )
                if owner == 0:
                    pl.when(jnp.logical_or(xl != xs, core != cs))(arrival.wait_recv)
                else:
                    arrival.wait_recv()
        if owner == 0:
            b_local(j, p).wait()

        def block(i, carry):
            lanes = pl.ds(pl.multiple_of(i * SPAN, SPAN), SPAN)
            at = (p, i // 8, lax.rem(i, 2), lax.rem(i // 2, 4))
            t = []
            for c in range(3):
                value = infl[at + (c,)]
                if p:
                    value = value + cols[c][:, :1] * psi[c, :, lanes]
                psi[c, :, lanes] = value
                t.append(value)
            f = [cols[3 + c][:, :1] for c in range(6)]
            v[0, p + 1, :, lanes] = cols[9][:, :1] + f[0] * t[0]
            v[1, p + 1, :, lanes] = f[1] * t[0] + f[2] * t[1]
            v[2, p + 1, :, lanes] = f[3] * t[0] + f[4] * t[1] + f[5] * t[2]
            return carry

        lax.fori_loop(0, COLS, block, 0)

    sub = lax.broadcasted_iota(jnp.int32, (NZ, WIDE), 0)
    chunks = NY // WIDE

    def section(stage, first, number):
        src = field[stage]
        half = 1.0 if stage == 0 else 0.5
        k_spread = TIME_STEP * VISCOSITY * half
        k_advect = TIME_STEP * 0.5 * half
        k_centre = half - 6.0 * k_spread

        def body(i, carry):
            x = first + i // chunks
            y = lax.rem(i, chunks)
            here = pl.ds(pl.multiple_of(y * WIDE, WIDE), WIDE)
            left = pl.ds(pl.multiple_of(lax.rem(y * WIDE + NY - 128, NY), 128), 128)
            right = pl.ds(pl.multiple_of(lax.rem(y * WIDE + WIDE, NY), 128), 128)
            centre = [src[c, x + 1, :, here] for c in range(3)]
            u = [k_advect * value for value in centre]
            to_next = [k_spread - value for value in u]
            to_prev = [k_spread + value for value in u]
            for c in range(3):
                mid_c = centre[c]
                y_prev = jnp.concatenate([src[c, x + 1, :, left], mid_c], axis=1)
                y_prev = pltpu.roll(y_prev, 1, 1)[:, 128:]
                y_next = jnp.concatenate([mid_c, src[c, x + 1, :, right]], axis=1)
                y_next = pltpu.roll(y_next, WIDE + 127, 1)[:, :WIDE]
                z_prev = jnp.where(sub == 0, hz[stage, 0, c, x, :, here], pltpu.roll(mid_c, 1, 0))
                z_next = jnp.where(
                    sub == NZ - 1, hz[stage, 1, c, x, :, here], pltpu.roll(mid_c, NZ - 1, 0)
                )
                total = k_centre * mid_c
                total = total + (to_next[0] * src[c, x + 2, :, here] + to_prev[0] * src[c, x, :, here])
                total = total + (to_next[1] * z_next + to_prev[1] * z_prev)
                total = total + (to_next[2] * y_next + to_prev[2] * y_prev)
                if stage == 0:
                    s[c, x + 1, :, here] = total
                else:
                    o[c, x, :, here] = total + 0.5 * v[c, x + 1, :, here]
            return carry

        lax.fori_loop(0, number * chunks, body, 0)

    def flush(n, first, number):
        return pltpu.make_async_copy(
            o.at[:, pl.ds(first, number)], out.at[:, pl.ds(first, number)], out_sem.at[n]
        )

    vel_load(1).wait()
    send_x(0, 0)
    send_z(0, 5)
    send_z(0, 4)

    @pl.when(r != 0)
    def _():
        vel_load(0).wait()
        x_face(0, 1).start()
        for n in range(4):
            send_z(0, n)

    each_slot(smooth)
    each_slot(forward)

    recv_z(0, 5)
    section(0, 12, 3)
    recv_z(0, 4)
    section(0, 9, 3)
    recv_x(0, 1)
    section(0, 15, 1)
    send_x(1, 0)
    send_z(1, 5)

    @pl.when(r == 0)
    def _():
        for p in range(PL):
            inflow(p)
            if p % 2 == 1:
                send_z(0, p // 2)

    recv_x(0, 0)
    recv_z(0, 0)
    section(0, 0, 1)
    send_x(1, 1)
    for n in range(4):
        if n < 3:
            recv_z(0, n + 1)
        section(0, GROUPS[n][0] + 1, 2)
        send_z(1, n)
    send_z(1, 4)

    recv_z(1, 5)
    section(1, 13, 2)
    flush(0, 13, 2).start()
    recv_z(1, 0)
    section(1, 1, 1)
    for n in range(1, 4):
        recv_z(1, n)
        section(1, GROUPS[n][0], 2)
    flush(1, 1, 7).start()
    recv_z(1, 4)
    section(1, 8, 5)
    flush(2, 8, 5).start()
    recv_x(1, 1)
    section(1, 15, 1)
    flush(3, 15, 1).start()
    recv_x(1, 0)
    section(1, 0, 1)
    flush(4, 0, 1).start()

    each_slot(forwarded)
    for stage in range(2):
        for n in range(NG):
            sent_z(stage, n)
        for side in range(2):
            sent_x(stage, side)
    flush(0, 13, 2).wait()
    flush(1, 1, 7).wait()
    flush(2, 8, 5).wait()
    flush(3, 15, 1).wait()
    flush(4, 0, 1).wait()


def local(velocity, noise, previous, decay, stress_factor, mean_profile):
    vmem = pl.BlockSpec(memory_space=pltpu.VMEM)
    hbm = pl.BlockSpec(memory_space=pl.ANY)
    dma = pltpu.SemaphoreType.DMA
    buffers = [
        (3, NX + 2, NZ, NY), (3, NX + 2, NZ, NY), (3, NX, NZ, NY), (2, 2, 3, NX, 1, NY),
        (SLOTS, 3, DEPTH, SPAN), (3, DEPTH, SPAN), (SLOTS, 2, DEPTH, 128), (SLOTS, 2, DEPTH, 128),
        (SLOTS, 3, 2, 4, 2, NZ, SPAN), (SLOTS, 4, 3, 2, 2, NZ, SPAN),
        (PL, 2, 2, 4, 3, NZ, SPAN), (3, NZ, NY), (10, NZ, 128), (3, DEPTH, 128),
    ]
    call = pl.pallas_call(
        kernel,
        out_shape=jax.ShapeDtypeStruct((3, NX, NZ, NY), F32),
        in_specs=[hbm, hbm, hbm] + [vmem] * 7,
        out_specs=hbm,
        scratch_shapes=[pltpu.VMEM(shape, F32) for shape in buffers]
        + [
            dma((SLOTS + 3,)), dma((SLOTS, 2)), dma((SLOTS, 2)), dma((SLOTS, 4)), dma((SLOTS, 4)),
            dma((SLOTS,)), dma((SLOTS, 2, 2)), dma((PL, 2, 2)), dma((SLOTS,)),
            dma((2, 2, NG)), dma((2, 2, NG)), dma((2, 2)), dma((2, 2)), dma((5,)),
        ],
        compiler_params=pltpu.CompilerParams(
            collective_id=0, has_side_effects=True, vmem_limit_bytes=58 * 2**20
        ),
        name="inflow_step",
    )
    return call(
        velocity, noise, previous, decay, stress_factor, mean_profile[None, :],
        *(jnp.asarray(w) for w in weights()),
    )


def solution(mesh):
    placed = (
        P(None, "grp", "gx", None),
        P(None, None, None, "gx"),
        P(None, None, "gx"),
        P(),
        P(),
        P(),
    )
    return jax.shard_map(
        local, mesh=mesh, in_specs=placed, out_specs=P(None, "grp", "gx", None), check_vma=False
    )
```

```python
import functools

import jax
import jax.numpy as jnp
import ml_dtypes
import numpy as np
from jax import lax
from jax.experimental import pallas as pl
from jax.experimental.pallas import tpu as pltpu
from jax.sharding import PartitionSpec as P

HALF = 32
TIME_STEP = 0.15
VISCOSITY = 0.2
PL = 8
ROWS, COLS = 8, 16
NX, NZ, NY = 16, 8, 4096
SPAN = NY // COLS
DEPTH = NZ * COLS
MESH = pl.DeviceIdType.MESH
F32, BF16 = jnp.float32, jnp.bfloat16

PLANES = {0: (0, 4, 6), 1: (1, 5), 3: (2, 7), 4: (3,)}
SLOTS = max(len(v) for v in PLANES.values())
OWNER = {p: (r, j) for r, v in PLANES.items() for j, p in enumerate(v)}

GROUPS = ((0, 2), (2, 2), (4, 2), (6, 2), (8, 1), (9, 3), (12, 3), (15, 1))
NG = len(GROUPS)


def weights():
    k = np.arange(-HALF, HALF + 1, dtype=np.float64)
    length = HALF / 2.0
    w = np.exp(-np.pi * k * k / (2.0 * length * length))
    w = w / np.sqrt(np.sum(w * w))

    def band(distance):
        inside = np.abs(distance) <= HALF
        return np.where(inside, w[np.clip(distance + HALF, 0, 2 * HALF)], 0.0)

    cols = np.arange(SPAN)[None, :]
    main = band(np.arange(SPAN)[:, None] - cols)
    wy = np.zeros((SPAN + 128, SPAN))
    wy[:SPAN] = main
    rim = np.arange(HALF)[:, None]
    wy[SPAN : SPAN + HALF] = band(rim - HALF - cols)
    wy[SPAN + HALF : SPAN + 2 * HALF] = band(rim + SPAN - cols)
    wz = band(np.arange(DEPTH)[:, None] - np.arange(DEPTH)[None, :])

    def split(a):
        a = a.astype(np.float32)
        hi = a.astype(ml_dtypes.bfloat16)
        lo = (a - hi.astype(np.float32)).astype(ml_dtypes.bfloat16)
        return hi, lo

    zh, zl = split(wz)
    return split(wy) + (np.concatenate([zh, zl]),)


def split_bf16(value):
    hi = value.astype(BF16)
    return hi, (value - hi.astype(F32)).astype(BF16)


def dot(a, b):
    return jnp.dot(a, b, preferred_element_type=F32)


def kernel(
    vel, noise, prev, decay, stress, mean, wyh, wyl, wz, o,
    v, s, hz, nz, pv, rim_out, rim_in, sm, mid, infl, psi, cols, dec,
    load_sem, rim_s, rim_r, a_s, a_r, b_s, b_r, b_l, z_s, z_r, x_s, x_r,
):
    r, g = lax.axis_index("grp"), lax.axis_index("gx")
    xl, z, core = g // 8, lax.rem(g // 2, 4), lax.rem(g, 2)

    def by_row(values, default):
        picked = jnp.int32(default)
        for row, value in values.items():
            picked = jnp.where(r == row, value, picked)
        return picked

    count = by_row({row: len(p) for row, p in PLANES.items()}, 0)
    plane_of = [
        by_row({row: (p[j] if j < len(p) else 0) for row, p in PLANES.items()}, 0)
        for j in range(SLOTS)
    ]
    up, down = lax.rem(g + 1, COLS), lax.rem(g + COLS - 1, COLS)

    def remote(src, dst, send, recv, row, col):
        return pltpu.make_async_remote_copy(
            src_ref=src, dst_ref=dst, send_sem=send, recv_sem=recv,
            device_id=(row, col), device_id_type=MESH,
        )

    def each_slot(body):
        for j in range(SLOTS):
            pl.when(j < count)(functools.partial(body, j))

    def noise_load(j):
        return pltpu.make_async_copy(noise.at[:, plane_of[j]], nz.at[j], load_sem.at[j])

    def prev_load():
        return pltpu.make_async_copy(prev, pv, load_sem.at[SLOTS])

    def vel_load(i):
        return pltpu.make_async_copy(
            vel.at[:, pl.ds(8 * i, 8)], v.at[:, pl.ds(1 + 8 * i, 8)], load_sem.at[SLOTS + 1 + i]
        )

    each_slot(lambda j: noise_load(j).start())
    pl.when(r == 0)(lambda: prev_load().start())
    vel_load(1).start()
    pl.when(r != 0)(lambda: vel_load(0).start())

    barrier = pltpu.get_barrier_semaphore()

    def greet(row, col):
        pl.semaphore_signal(barrier, 1, device_id=(row, col), device_id_type=MESH)

    greet(r, up)
    greet(r, down)
    pl.when(r > 0)(lambda: greet(r - 1, g))
    pl.when(r < ROWS - 1)(lambda: greet(r + 1, g))

    @pl.when(count > 0)
    def _():
        for k in (1, 2, 3):
            greet(r, xl * 8 + lax.rem(z + k, 4) * 2 + core)

    @pl.when(r == 0)
    def _():
        for row in PLANES:
            for xs in range(2):
                for cs in range(2):
                    if row == 0:
                        @pl.when(jnp.logical_or(xs != xl, cs != core))
                        def _():
                            greet(row, xs * 8 + z * 2 + cs)
                    else:
                        greet(row, xs * 8 + z * 2 + cs)

    row_i = lax.broadcasted_iota(jnp.int32, (NZ, 128), 0)
    lane_i = lax.broadcasted_iota(jnp.int32, (NZ, 128), 1)

    @pl.when(r == 0)
    def _():
        mine = lane_i == row_i + NZ * g

        def column(row):
            picked = jnp.where(mine, row, 0.0)
            return jnp.broadcast_to(jnp.sum(picked, axis=1, keepdims=True), (NZ, 128))

        for c in range(3):
            cols[c] = column(decay[c : c + 1, :])
        for c in range(6):
            cols[3 + c] = column(stress[c : c + 1, :])
        cols[9] = column(mean[...])

    @pl.when(count > 0)
    def _():
        row_d = lax.broadcasted_iota(jnp.int32, (DEPTH, 128), 0)
        lane_d = lax.broadcasted_iota(jnp.int32, (DEPTH, 128), 1)
        for c in range(3):
            picked = jnp.where(row_d == lane_d, decay[c : c + 1, :], 0.0)
            dec[c] = jnp.broadcast_to(jnp.sum(picked, axis=1, keepdims=True), (DEPTH, 128))

    @pl.when(g == 0)
    def _():
        hz[0, 0] = jnp.zeros(hz.shape[2:], F32)
        hz[1, 0] = jnp.zeros(hz.shape[2:], F32)

    @pl.when(g == COLS - 1)
    def _():
        hz[0, 1] = jnp.zeros(hz.shape[2:], F32)
        hz[1, 1] = jnp.zeros(hz.shape[2:], F32)

    def clear_x(at):
        for c in range(3):
            v[c, at] = jnp.zeros((NZ, NY), F32)
            s[c, at] = jnp.zeros((NZ, NY), F32)

    pl.when(r == 0)(lambda: clear_x(0))
    pl.when(r == ROWS - 1)(lambda: clear_x(NX + 1))

    def pack(j):
        noise_load(j).wait()
        lane = lax.broadcasted_iota(jnp.int32, (DEPTH, 128), 1)
        high = jnp.zeros((DEPTH, 128), F32)
        low = jnp.zeros((DEPTH, 128), F32)
        for c in range(3):
            here = jnp.logical_and(lane >= HALF * c, lane < HALF * (c + 1))
            last = nz[j, c, :, SPAN - 128 :]
            first = nz[j, c, :, :128]
            high = jnp.where(here, pltpu.roll(last, (HALF * c + HALF) % 128, 1), high)
            low = jnp.where(here, pltpu.roll(first, HALF * c, 1) if c else first, low)
        rim_out[j, 0] = high
        rim_out[j, 1] = low

    each_slot(pack)

    waits = 2 + (r > 0).astype(jnp.int32) + (r < ROWS - 1).astype(jnp.int32)
    waits = waits + jnp.where(count > 0, 7, 0) - (r == 0).astype(jnp.int32)
    pl.semaphore_wait(barrier, waits)

    def rims(j):
        return (
            remote(rim_out.at[j, 0], rim_in.at[j, 0], rim_s.at[j, 0], rim_r.at[j, 0], r, up),
            remote(rim_out.at[j, 1], rim_in.at[j, 1], rim_s.at[j, 1], rim_r.at[j, 1], r, down),
        )

    def send_rims(j):
        for copy in rims(j):
            copy.start()

    each_slot(send_rims)

    field = (v, s)

    def z_face(stage, n, side):
        first, width = GROUPS[n]
        row = NZ - 1 if side == 0 else 0
        return remote(
            field[stage].at[:, pl.ds(1 + first, width), row],
            hz.at[stage, side, :, pl.ds(first, width), 0],
            z_s.at[stage, side, n], z_r.at[stage, side, n], r, up if side == 0 else down,
        )

    def send_z(stage, n):
        pl.when(g < COLS - 1)(lambda: z_face(stage, n, 0).start())
        pl.when(g > 0)(lambda: z_face(stage, n, 1).start())

    def recv_z(stage, n):
        pl.when(g > 0)(lambda: z_face(stage, n, 0).wait_recv())
        pl.when(g < COLS - 1)(lambda: z_face(stage, n, 1).wait_recv())

    def sent_z(stage, n):
        pl.when(g < COLS - 1)(lambda: z_face(stage, n, 0).wait_send())
        pl.when(g > 0)(lambda: z_face(stage, n, 1).wait_send())

    def x_face(stage, side):
        src, dst, row = (NX, 0, r + 1) if side == 0 else (1, NX + 1, r - 1)
        return remote(
            field[stage].at[:, src], field[stage].at[:, dst],
            x_s.at[stage, side], x_r.at[stage, side], row, g,
        )

    def send_x(stage, side):
        pl.when(r < ROWS - 1 if side == 0 else r > 0)(lambda: x_face(stage, side).start())

    def sent_x(stage, side):
        pl.when(r < ROWS - 1 if side == 0 else r > 0)(lambda: x_face(stage, side).wait_send())

    def recv_x(stage, side):
        pl.when(r > 0 if side == 0 else r < ROWS - 1)(lambda: x_face(stage, side).wait_recv())

    def a_copy(j, k):
        there = lax.rem(z + k, 4)
        return remote(
            sm.at[j, :, :, there], mid.at[j, z], a_s.at[j, k], a_r.at[j, k],
            r, xl * 8 + there * 2 + core,
        )

    def smooth(j):
        for copy in rims(j):
            copy.wait_recv()
        lane = lax.broadcasted_iota(jnp.int32, (DEPTH, 128), 1)
        low, high = rim_in[j, 0], rim_in[j, 1]
        rows = []
        for c in range(3):
            before = pltpu.roll(low, (128 - HALF * c) % 128, 1) if c else low
            after = pltpu.roll(high, (128 + HALF - HALF * c) % 128, 1) if c != 1 else high
            rim = jnp.where(lane < HALF, before, jnp.where(lane < 2 * HALF, after, 0.0))
            rows.append(jnp.concatenate([nz[j, c], rim], axis=1))
        hi, lo = split_bf16(jnp.concatenate(rows, axis=0))
        both = dot(jnp.concatenate([hi, lo], axis=0), wyh[...])
        along_y = (both[: 3 * DEPTH] + both[3 * DEPTH :]) + dot(hi, wyl[...])
        for c in range(3):
            hi, lo = split_bf16(along_y[DEPTH * c : DEPTH * (c + 1)])
            both = dot(wz[...], hi)
            done = (both[:DEPTH] + both[DEPTH:]) + dot(wz[:DEPTH], lo)
            d = dec[c][:, :1]
            done = jnp.sqrt(1.0 - d * d) * done
            sm[j, c] = done.reshape(2, 4, 2, NZ, SPAN)
        if j == 0:
            @pl.when(r == 0)
            def _():
                prev_load().wait()
                for c in range(3):
                    first = sm[j, c].reshape(DEPTH, SPAN) + dec[c][:, :1] * pv[c]
                    sm[j, c] = first.reshape(2, 4, 2, NZ, SPAN)
        for k in (2, 1, 3):
            a_copy(j, k).start()
        pass_on(j, 0)

    def b_copy(j, k, xd, cd):
        here = lax.rem(z + k, 4)
        src = mid.at[j, here, :, xd, cd] if k else sm.at[j, :, xd, z, cd]
        return remote(
            src, infl.at[plane_of[j], xl, core, here], b_s.at[j, xd, cd],
            b_r.at[plane_of[j], xl, core], 0, xd * 8 + z * 2 + cd,
        )

    def b_local(j, k):
        here = lax.rem(z + k, 4)
        src = mid.at[j, here, :, xl, core] if k else sm.at[j, :, xl, z, core]
        return pltpu.make_async_copy(src, infl.at[plane_of[j], xl, core, here], b_l.at[j])

    def leaving(xd, cd):
        return jnp.logical_or(r != 0, jnp.logical_or(xl != xd, core != cd))

    def pass_on(j, k):
        for xd in range(2):
            for cd in range(2):
                pl.when(leaving(xd, cd))(lambda: b_copy(j, k, xd, cd).start())
        pl.when(r == 0)(lambda: b_local(j, k).start())

    def forward(j):
        for k in (1, 3, 2):
            a_copy(j, (4 - k) % 4).wait_recv()
            pass_on(j, k)

    def forwarded(j):
        for xd in range(2):
            for cd in range(2):
                whole = remote(
                    mid.at[j, :, :, 0, 0], infl.at[0, 0, 0], b_s.at[j, xd, cd], b_r.at[0, 0, 0],
                    0, xd * 8 + z * 2 + cd,
                )
                pl.when(leaving(xd, cd))(whole.wait_send)
        for k in (1, 2, 3):
            a_copy(j, k).wait_send()
        for copy in rims(j):
            copy.wait_send()

    def inflow(p):
        owner, j = OWNER[p]
        for xs in range(2):
            for cs in range(2):
                arrival = remote(
                    mid.at[j, :, :, 0, 0], infl.at[p, xs, cs], b_s.at[0, 0, 0], b_r.at[p, xs, cs],
                    0, xs * 8 + z * 2 + cs,
                )
                if owner == 0:
                    pl.when(jnp.logical_or(xl != xs, core != cs))(arrival.wait_recv)
                else:
                    arrival.wait_recv()
        if owner == 0:
            pltpu.make_async_copy(mid.at[j, :, :, 0, 0], infl.at[p, 0, 0], b_l.at[j]).wait()

        def block(i, carry):
            lanes = pl.ds(pl.multiple_of(i * SPAN, SPAN), SPAN)
            at = (p, i // 8, lax.rem(i, 2), lax.rem(i // 2, 4))
            t = []
            for c in range(3):
                value = infl[at + (c,)]
                if p:
                    value = value + cols[c][:, :1] * psi[c, :, lanes]
                psi[c, :, lanes] = value
                t.append(value)
            f = [cols[3 + c][:, :1] for c in range(6)]
            v[0, p + 1, :, lanes] = cols[9][:, :1] + f[0] * t[0]
            v[1, p + 1, :, lanes] = f[1] * t[0] + f[2] * t[1]
            v[2, p + 1, :, lanes] = f[3] * t[0] + f[4] * t[1] + f[5] * t[2]
            return carry

        lax.fori_loop(0, COLS, block, 0, unroll=8)

    sub = lax.broadcasted_iota(jnp.int32, (NZ, NY), 0)

    def section(stage, first, number):
        src = field[stage]
        half = 1.0 if stage == 0 else 0.5
        k_spread = TIME_STEP * VISCOSITY * half
        k_advect = TIME_STEP * 0.5 * half
        k_centre = half - 6.0 * k_spread

        def body(i, carry):
            x = first + i
            centre = [src[c, x + 1] for c in range(3)]
            u = [k_advect * value for value in centre]
            to_next = [k_spread - value for value in u]
            to_prev = [k_spread + value for value in u]
            for c in range(3):
                mid_c = centre[c]
                y_prev, y_next = pltpu.roll(mid_c, 1, 1), pltpu.roll(mid_c, NY - 1, 1)
                z_prev = jnp.where(sub == 0, hz[stage, 0, c, x], pltpu.roll(mid_c, 1, 0))
                z_next = jnp.where(sub == NZ - 1, hz[stage, 1, c, x], pltpu.roll(mid_c, NZ - 1, 0))
                total = k_centre * mid_c
                total = total + (to_next[0] * src[c, x + 2] + to_prev[0] * src[c, x])
                total = total + (to_next[1] * z_next + to_prev[1] * z_prev)
                total = total + (to_next[2] * y_next + to_prev[2] * y_prev)
                if stage == 0:
                    s[c, x + 1] = total
                else:
                    o[c, x] = total + 0.5 * v[c, x + 1]
            return carry

        lax.fori_loop(0, number, body, 0)

    def start_faces():
        for n in range(4):
            send_z(0, n)

    @pl.when(r != 0)
    def _():
        vel_load(0).wait()
        x_face(0, 1).start()

    vel_load(1).wait()
    send_x(0, 0)
    for n in (6, 5, 4, 7):
        send_z(0, n)
    pl.when(count == 0)(start_faces)
    each_slot(smooth)
    pl.when(jnp.logical_and(count > 0, r != 0))(start_faces)
    each_slot(forward)

    recv_z(0, 6)
    section(0, 12, 3)
    send_z(1, 6)
    recv_z(0, 5)
    section(0, 9, 3)
    send_z(1, 5)
    recv_z(0, 7)
    recv_x(0, 1)
    section(0, 15, 1)
    send_x(1, 0)
    send_z(1, 7)

    def arrive(*planes):
        @pl.when(r == 0)
        def _():
            for p in planes:
                inflow(p)
                if p % 2 == 1:
                    send_z(0, p // 2)

    def upper():
        recv_z(1, 6)
        recv_z(1, 5)
        section(1, 10, 4)
        recv_z(1, 7)
        section(1, 14, 1)

    pl.when(r == 0)(upper)
    arrive(0, 1, 2, 3)
    recv_x(0, 0)
    recv_z(0, 0)
    section(0, 0, 2)
    send_x(1, 1)
    recv_z(0, 1)
    section(0, 2, 1)
    send_z(1, 0)
    arrive(4, 5)
    section(0, 3, 1)
    send_z(1, 1)
    arrive(6, 7)
    recv_z(0, 2)
    section(0, 4, 2)
    send_z(1, 2)
    recv_z(0, 3)
    recv_z(0, 4)
    section(0, 6, 3)
    send_z(1, 3)
    send_z(1, 4)

    pl.when(r != 0)(upper)
    recv_z(1, 0)
    section(1, 1, 1)
    recv_z(1, 1)
    recv_z(1, 2)
    section(1, 2, 3)
    recv_x(1, 0)
    section(1, 0, 1)
    recv_x(1, 1)
    section(1, 15, 1)
    recv_z(1, 3)
    recv_z(1, 4)
    section(1, 5, 5)

    each_slot(forwarded)
    for stage in range(2):
        for n in range(NG):
            sent_z(stage, n)
        for side in range(2):
            sent_x(stage, side)


def store(src, dst, sem):
    copies = []
    for c in range(3):
        for i in range(4):
            part = pl.ds(4 * i, 4)
            copies.append(pltpu.make_async_copy(src.at[c, part], dst.at[c, part], sem.at[c, i]))
    for copy in copies:
        copy.start()
    for copy in copies:
        copy.wait()


def local(velocity, noise, previous, decay, stress_factor, mean_profile):
    vmem = pl.BlockSpec(memory_space=pltpu.VMEM)
    hbm = pl.BlockSpec(memory_space=pl.ANY)
    dma = pltpu.SemaphoreType.DMA
    buffers = [
        (3, NX + 2, NZ, NY), (3, NX + 2, NZ, NY), (2, 2, 3, NX, 1, NY),
        (SLOTS, 3, DEPTH, SPAN), (3, DEPTH, SPAN), (SLOTS, 2, DEPTH, 128), (SLOTS, 2, DEPTH, 128),
        (SLOTS, 3, 2, 4, 2, NZ, SPAN), (SLOTS, 4, 3, 2, 2, NZ, SPAN),
        (PL, 2, 2, 4, 3, NZ, SPAN), (3, NZ, NY), (10, NZ, 128), (3, DEPTH, 128),
    ]
    call = pl.pallas_call(
        kernel,
        out_shape=pltpu.VMEM((3, NX, NZ, NY), F32),
        in_specs=[hbm, hbm, hbm] + [vmem] * 6,
        out_specs=vmem,
        scratch_shapes=[pltpu.VMEM(shape, F32) for shape in buffers]
        + [
            dma((SLOTS + 3,)), dma((SLOTS, 2)), dma((SLOTS, 2)), dma((SLOTS, 4)), dma((SLOTS, 4)),
            dma((SLOTS, 2, 2)), dma((PL, 2, 2)), dma((SLOTS,)),
            dma((2, 2, NG)), dma((2, 2, NG)), dma((2, 2)), dma((2, 2)),
        ],
        compiler_params=pltpu.CompilerParams(
            collective_id=0, has_side_effects=True, vmem_limit_bytes=48 * 2**20
        ),
        name="inflow_step",
    )
    done = call(
        velocity, noise, previous, decay, stress_factor, mean_profile[None, :],
        *(jnp.asarray(w) for w in weights()),
    )
    return pl.pallas_call(
        store,
        out_shape=jax.ShapeDtypeStruct(done.shape, F32),
        in_specs=[vmem],
        out_specs=hbm,
        scratch_shapes=[dma((3, 4))],
        compiler_params=pltpu.CompilerParams(vmem_limit_bytes=2**20),
        name="store",
    )(done)


def solution(mesh):
    placed = (
        P(None, "grp", "gx", None),
        P(None, None, None, "gx"),
        P(None, None, "gx"),
        P(),
        P(),
        P(),
    )
    return jax.shard_map(
        local, mesh=mesh, in_specs=placed, out_specs=P(None, "grp", "gx", None), check_vma=False
    )
```

```python
import functools

import jax
import jax.numpy as jnp
import ml_dtypes
import numpy as np
from jax import lax
from jax.experimental import pallas as pl
from jax.experimental.pallas import tpu as pltpu
from jax.sharding import PartitionSpec as P

HALF = 32
TIME_STEP = 0.15
VISCOSITY = 0.2
PL = 8
ROWS, COLS = 8, 16
NX, NZ, NY = 16, 8, 4096
SPAN = NY // COLS
DEPTH = NZ * COLS
MESH = pl.DeviceIdType.MESH
F32, BF16 = jnp.float32, jnp.bfloat16

PAIR = 4
PLANES = {0: (0, 1, 4, 6), PAIR: (0, 1, 4, 6), 1: (3, 7), 3: (2, 5)}
SLOTS = max(len(v) for v in PLANES.values())
OWNER = {p: (r, j) for r, v in PLANES.items() if r != PAIR for j, p in enumerate(v)}

GROUPS = ((0, 2), (2, 2), (4, 2), (6, 2), (8, 1), (9, 3), (12, 3), (15, 1))
NG = len(GROUPS)


def weights():
    k = np.arange(-HALF, HALF + 1, dtype=np.float64)
    length = HALF / 2.0
    w = np.exp(-np.pi * k * k / (2.0 * length * length))
    w = w / np.sqrt(np.sum(w * w))

    def band(distance):
        inside = np.abs(distance) <= HALF
        return np.where(inside, w[np.clip(distance + HALF, 0, 2 * HALF)], 0.0)

    cols = np.arange(SPAN)[None, :]
    main = band(np.arange(SPAN)[:, None] - cols)
    wy = np.zeros((SPAN + 128, SPAN))
    wy[:SPAN] = main
    rim = np.arange(HALF)[:, None]
    wy[SPAN : SPAN + HALF] = band(rim - HALF - cols)
    wy[SPAN + HALF : SPAN + 2 * HALF] = band(rim + SPAN - cols)
    wz = band(np.arange(DEPTH)[:, None] - np.arange(DEPTH)[None, :])

    def split(a):
        a = a.astype(np.float32)
        hi = a.astype(ml_dtypes.bfloat16)
        lo = (a - hi.astype(np.float32)).astype(ml_dtypes.bfloat16)
        return hi, lo

    zh, zl = split(wz)
    return split(wy) + (np.concatenate([zh, zl]),)


def split_bf16(value):
    hi = value.astype(BF16)
    return hi, (value - hi.astype(F32)).astype(BF16)


def dot(a, b):
    return jnp.dot(a, b, preferred_element_type=F32)


def kernel(
    vel, noise, prev, decay, stress, mean, wyh, wyl, wz, o,
    v, s, hz, nz, pv, rim_out, rim_in, sm, mid, infl, psi, cols, dec,
    load_sem, rim_s, rim_r, a_s, a_r, b_s, b_r, b_l, z_s, z_r, x_s, x_r,
):
    r, g = lax.axis_index("grp"), lax.axis_index("gx")
    xl, z, core = g // 8, lax.rem(g // 2, 4), lax.rem(g, 2)

    def by_row(values, default):
        picked = jnp.int32(default)
        for row, value in values.items():
            picked = jnp.where(r == row, value, picked)
        return picked

    count = by_row({row: len(p) for row, p in PLANES.items()}, 0)
    plane_of = [
        by_row({row: (p[j] if j < len(p) else 0) for row, p in PLANES.items()}, 0)
        for j in range(SLOTS)
    ]
    up, down = lax.rem(g + 1, COLS), lax.rem(g + COLS - 1, COLS)

    def remote(src, dst, send, recv, row, col):
        return pltpu.make_async_remote_copy(
            src_ref=src, dst_ref=dst, send_sem=send, recv_sem=recv,
            device_id=(row, col), device_id_type=MESH,
        )

    def each_slot(body):
        for j in range(SLOTS):
            pl.when(j < count)(functools.partial(body, j))

    def noise_load(j):
        return pltpu.make_async_copy(noise.at[:, plane_of[j]], nz.at[j], load_sem.at[j])

    def prev_load():
        return pltpu.make_async_copy(prev, pv, load_sem.at[SLOTS])

    def vel_load(i):
        return pltpu.make_async_copy(
            vel.at[:, pl.ds(8 * i, 8)], v.at[:, pl.ds(1 + 8 * i, 8)], load_sem.at[SLOTS + 1 + i]
        )

    each_slot(lambda j: noise_load(j).start())
    first_plane = jnp.logical_or(r == 0, r == PAIR)
    pl.when(first_plane)(lambda: prev_load().start())
    vel_load(1).start()
    pl.when(r != 0)(lambda: vel_load(0).start())

    barrier = pltpu.get_barrier_semaphore()

    def greet(row, col):
        pl.semaphore_signal(barrier, 1, device_id=(row, col), device_id_type=MESH)

    greet(r, up)
    greet(r, down)
    pl.when(r > 0)(lambda: greet(r - 1, g))
    pl.when(r < ROWS - 1)(lambda: greet(r + 1, g))

    @pl.when(count > 0)
    def _():
        for k in (1, 2, 3):
            greet(r, xl * 8 + lax.rem(z + k, 4) * 2 + core)

    @pl.when(r == 0)
    def _():
        for cs in range(2):
            for row in PLANES:
                if row == 0:
                    pl.when(core != cs)(lambda: greet(row, xl * 8 + z * 2 + cs))
                elif row == PAIR:
                    greet(row, (1 - xl) * 8 + z * 2 + cs)
                else:
                    greet(row, z * 2 + cs)
                    greet(row, 8 + z * 2 + cs)

    row_i = lax.broadcasted_iota(jnp.int32, (NZ, 128), 0)
    lane_i = lax.broadcasted_iota(jnp.int32, (NZ, 128), 1)

    @pl.when(r == 0)
    def _():
        mine = lane_i == row_i + NZ * g

        def column(row):
            picked = jnp.where(mine, row, 0.0)
            return jnp.broadcast_to(jnp.sum(picked, axis=1, keepdims=True), (NZ, 128))

        for c in range(3):
            cols[c] = column(decay[c : c + 1, :])
        for c in range(6):
            cols[3 + c] = column(stress[c : c + 1, :])
        cols[9] = column(mean[...])

    @pl.when(count > 0)
    def _():
        row_d = lax.broadcasted_iota(jnp.int32, (DEPTH, 128), 0)
        lane_d = lax.broadcasted_iota(jnp.int32, (DEPTH, 128), 1)
        for c in range(3):
            picked = jnp.where(row_d == lane_d, decay[c : c + 1, :], 0.0)
            dec[c] = jnp.broadcast_to(jnp.sum(picked, axis=1, keepdims=True), (DEPTH, 128))

    @pl.when(g == 0)
    def _():
        hz[0, 0] = jnp.zeros(hz.shape[2:], F32)
        hz[1, 0] = jnp.zeros(hz.shape[2:], F32)

    @pl.when(g == COLS - 1)
    def _():
        hz[0, 1] = jnp.zeros(hz.shape[2:], F32)
        hz[1, 1] = jnp.zeros(hz.shape[2:], F32)

    def clear_x(at):
        for c in range(3):
            v[c, at] = jnp.zeros((NZ, NY), F32)
            s[c, at] = jnp.zeros((NZ, NY), F32)

    pl.when(r == 0)(lambda: clear_x(0))
    pl.when(r == ROWS - 1)(lambda: clear_x(NX + 1))

    def pack(j):
        noise_load(j).wait()
        lane = lax.broadcasted_iota(jnp.int32, (DEPTH, 128), 1)
        high = jnp.zeros((DEPTH, 128), F32)
        low = jnp.zeros((DEPTH, 128), F32)
        for c in range(3):
            here = jnp.logical_and(lane >= HALF * c, lane < HALF * (c + 1))
            last = nz[j, c, :, SPAN - 128 :]
            first = nz[j, c, :, :128]
            high = jnp.where(here, pltpu.roll(last, (HALF * c + HALF) % 128, 1), high)
            low = jnp.where(here, pltpu.roll(first, HALF * c, 1) if c else first, low)
        rim_out[j, 0] = high
        rim_out[j, 1] = low

    each_slot(pack)

    waits = 2 + (r > 0).astype(jnp.int32) + (r < ROWS - 1).astype(jnp.int32)
    waits = waits + by_row({0: 4, PAIR: 5, 1: 7, 3: 7}, 0)
    pl.semaphore_wait(barrier, waits)

    def rims(j):
        return (
            remote(rim_out.at[j, 0], rim_in.at[j, 0], rim_s.at[j, 0], rim_r.at[j, 0], r, up),
            remote(rim_out.at[j, 1], rim_in.at[j, 1], rim_s.at[j, 1], rim_r.at[j, 1], r, down),
        )

    def send_rims(j):
        for copy in rims(j):
            copy.start()

    each_slot(send_rims)

    field = (v, s)

    def z_face(stage, n, side):
        first, width = GROUPS[n]
        row = NZ - 1 if side == 0 else 0
        return remote(
            field[stage].at[:, pl.ds(1 + first, width), row],
            hz.at[stage, side, :, pl.ds(first, width), 0],
            z_s.at[stage, side, n], z_r.at[stage, side, n], r, up if side == 0 else down,
        )

    def send_z(stage, n):
        pl.when(g < COLS - 1)(lambda: z_face(stage, n, 0).start())
        pl.when(g > 0)(lambda: z_face(stage, n, 1).start())

    def recv_z(stage, n):
        pl.when(g > 0)(lambda: z_face(stage, n, 0).wait_recv())
        pl.when(g < COLS - 1)(lambda: z_face(stage, n, 1).wait_recv())

    def sent_z(stage, n):
        pl.when(g < COLS - 1)(lambda: z_face(stage, n, 0).wait_send())
        pl.when(g > 0)(lambda: z_face(stage, n, 1).wait_send())

    def x_face(stage, side):
        src, dst, row = (NX, 0, r + 1) if side == 0 else (1, NX + 1, r - 1)
        return remote(
            field[stage].at[:, src], field[stage].at[:, dst],
            x_s.at[stage, side], x_r.at[stage, side], row, g,
        )

    def send_x(stage, side):
        pl.when(r < ROWS - 1 if side == 0 else r > 0)(lambda: x_face(stage, side).start())

    def sent_x(stage, side):
        pl.when(r < ROWS - 1 if side == 0 else r > 0)(lambda: x_face(stage, side).wait_send())

    def recv_x(stage, side):
        pl.when(r > 0 if side == 0 else r < ROWS - 1)(lambda: x_face(stage, side).wait_recv())

    def for_side(xd, body):
        across = xl != xd
        used = jnp.where(r == 0, jnp.logical_not(across), jnp.where(r == PAIR, across, True))
        pl.when(used)(body)

    def a_copy(j, k, xd):
        there = lax.rem(z + k, 4)
        return remote(
            sm.at[j, :, xd, there], mid.at[j, xd, z], a_s.at[j, k, xd], a_r.at[j, k, xd],
            r, xl * 8 + there * 2 + core,
        )

    def smooth(j):
        for copy in rims(j):
            copy.wait_recv()
        lane = lax.broadcasted_iota(jnp.int32, (DEPTH, 128), 1)
        low, high = rim_in[j, 0], rim_in[j, 1]
        rows = []
        for c in range(3):
            before = pltpu.roll(low, (128 - HALF * c) % 128, 1) if c else low
            after = pltpu.roll(high, (128 + HALF - HALF * c) % 128, 1) if c != 1 else high
            rim = jnp.where(lane < HALF, before, jnp.where(lane < 2 * HALF, after, 0.0))
            rows.append(jnp.concatenate([nz[j, c], rim], axis=1))
        hi, lo = split_bf16(jnp.concatenate(rows, axis=0))
        both = dot(jnp.concatenate([hi, lo], axis=0), wyh[...])
        along_y = (both[: 3 * DEPTH] + both[3 * DEPTH :]) + dot(hi, wyl[...])
        for c in range(3):
            hi, lo = split_bf16(along_y[DEPTH * c : DEPTH * (c + 1)])
            both = dot(wz[...], hi)
            done = (both[:DEPTH] + both[DEPTH:]) + dot(wz[:DEPTH], lo)
            d = dec[c][:, :1]
            done = jnp.sqrt(1.0 - d * d) * done
            sm[j, c] = done.reshape(2, 4, 2, NZ, SPAN)
        if j == 0:
            @pl.when(first_plane)
            def _():
                prev_load().wait()
                for c in range(3):
                    first = sm[j, c].reshape(DEPTH, SPAN) + dec[c][:, :1] * pv[c]
                    sm[j, c] = first.reshape(2, 4, 2, NZ, SPAN)
        for k in (2, 1, 3):
            for xd in range(2):
                for_side(xd, lambda: a_copy(j, k, xd).start())
        pass_on(j, 0)

    def b_copy(j, k, xd, cd):
        here = lax.rem(z + k, 4)
        src = mid.at[j, xd, here, :, cd] if k else sm.at[j, :, xd, z, cd]
        return remote(
            src, infl.at[plane_of[j], xl, core, here], b_s.at[j, xd, cd],
            b_r.at[plane_of[j], xl, core], 0, xd * 8 + z * 2 + cd,
        )

    def b_local(j, k):
        here = lax.rem(z + k, 4)
        src = mid.at[j, xl, here, :, core] if k else sm.at[j, :, xl, z, core]
        return pltpu.make_async_copy(src, infl.at[plane_of[j], xl, core, here], b_l.at[j])

    def leaving(cd):
        return jnp.logical_or(r != 0, core != cd)

    def pass_on(j, k):
        for xd in range(2):
            @functools.partial(for_side, xd)
            def _():
                for cd in range(2):
                    pl.when(leaving(cd))(lambda: b_copy(j, k, xd, cd).start())
        pl.when(r == 0)(lambda: b_local(j, k).start())

    def forward(j):
        for k in (1, 3, 2):
            for xd in range(2):
                for_side(xd, lambda: a_copy(j, (4 - k) % 4, xd).wait_recv())
            pass_on(j, k)

    def forwarded(j):
        for xd in range(2):
            @functools.partial(for_side, xd)
            def _():
                for cd in range(2):
                    whole = remote(
                        mid.at[j, 0, :, :, 0], infl.at[0, 0, 0], b_s.at[j, xd, cd],
                        b_r.at[0, 0, 0], 0, xd * 8 + z * 2 + cd,
                    )
                    pl.when(leaving(cd))(whole.wait_send)
                for k in (1, 2, 3):
                    a_copy(j, k, xd).wait_send()
        for copy in rims(j):
            copy.wait_send()

    def inflow(p):
        owner, j = OWNER[p]
        for xs in range(2):
            for cs in range(2):
                arrival = remote(
                    mid.at[j, 0, :, :, 0], infl.at[p, xs, cs], b_s.at[0, 0, 0], b_r.at[p, xs, cs],
                    0, xs * 8 + z * 2 + cs,
                )
                if owner == 0:
                    pl.when(jnp.logical_or(xl != xs, core != cs))(arrival.wait_recv)
                else:
                    arrival.wait_recv()
        if owner == 0:
            pltpu.make_async_copy(mid.at[j, 0, :, :, 0], infl.at[p, 0, 0], b_l.at[j]).wait()

        def block(i, carry):
            lanes = pl.ds(pl.multiple_of(i * SPAN, SPAN), SPAN)
            at = (p, i // 8, lax.rem(i, 2), lax.rem(i // 2, 4))
            t = []
            for c in range(3):
                value = infl[at + (c,)]
                if p:
                    value = value + cols[c][:, :1] * psi[c, :, lanes]
                psi[c, :, lanes] = value
                t.append(value)
            f = [cols[3 + c][:, :1] for c in range(6)]
            v[0, p + 1, :, lanes] = cols[9][:, :1] + f[0] * t[0]
            v[1, p + 1, :, lanes] = f[1] * t[0] + f[2] * t[1]
            v[2, p + 1, :, lanes] = f[3] * t[0] + f[4] * t[1] + f[5] * t[2]
            return carry

        lax.fori_loop(0, COLS, block, 0, unroll=8)

    sub = lax.broadcasted_iota(jnp.int32, (NZ, NY), 0)

    def section(stage, first, number):
        src = field[stage]
        half = 1.0 if stage == 0 else 0.5
        k_spread = TIME_STEP * VISCOSITY * half
        k_advect = TIME_STEP * 0.5 * half
        k_centre = half - 6.0 * k_spread

        def body(i, carry):
            x = first + i
            centre = [src[c, x + 1] for c in range(3)]
            u = [k_advect * value for value in centre]
            to_next = [k_spread - value for value in u]
            to_prev = [k_spread + value for value in u]
            for c in range(3):
                mid_c = centre[c]
                y_prev, y_next = pltpu.roll(mid_c, 1, 1), pltpu.roll(mid_c, NY - 1, 1)
                z_prev = jnp.where(sub == 0, hz[stage, 0, c, x], pltpu.roll(mid_c, 1, 0))
                z_next = jnp.where(sub == NZ - 1, hz[stage, 1, c, x], pltpu.roll(mid_c, NZ - 1, 0))
                total = k_centre * mid_c
                total = total + (to_next[0] * src[c, x + 2] + to_prev[0] * src[c, x])
                total = total + (to_next[1] * z_next + to_prev[1] * z_prev)
                total = total + (to_next[2] * y_next + to_prev[2] * y_prev)
                if stage == 0:
                    s[c, x + 1] = total
                else:
                    o[c, x] = total + 0.5 * v[c, x + 1]
            return carry

        lax.fori_loop(0, number, body, 0)

    def start_faces():
        for n in range(4):
            send_z(0, n)

    @pl.when(r != 0)
    def _():
        vel_load(0).wait()
        x_face(0, 1).start()

    vel_load(1).wait()
    send_x(0, 0)
    for n in (6, 5, 4, 7):
        send_z(0, n)
    pl.when(count == 0)(start_faces)
    each_slot(smooth)
    pl.when(jnp.logical_and(count > 0, r != 0))(start_faces)
    each_slot(forward)

    recv_z(0, 6)
    section(0, 12, 3)
    send_z(1, 6)
    recv_z(0, 5)
    section(0, 9, 3)
    send_z(1, 5)
    recv_z(0, 7)
    recv_x(0, 1)
    section(0, 15, 1)
    send_x(1, 0)
    send_z(1, 7)

    def arrive(*planes):
        @pl.when(r == 0)
        def _():
            for p in planes:
                inflow(p)
                if p % 2 == 1:
                    send_z(0, p // 2)

    def upper():
        recv_z(1, 6)
        recv_z(1, 5)
        section(1, 10, 4)
        recv_z(1, 7)
        section(1, 14, 1)

    pl.when(r == 0)(upper)
    arrive(0, 1, 2, 3)
    recv_x(0, 0)
    recv_z(0, 0)
    section(0, 0, 2)
    pl.when(r != 0)(lambda: each_slot(forwarded))
    send_x(1, 1)
    recv_z(0, 1)
    section(0, 2, 1)
    send_z(1, 0)
    arrive(4, 5)
    section(0, 3, 1)
    send_z(1, 1)
    arrive(6, 7)
    recv_z(0, 2)
    section(0, 4, 2)
    send_z(1, 2)
    recv_z(0, 3)
    recv_z(0, 4)
    section(0, 6, 3)
    send_z(1, 3)
    send_z(1, 4)

    pl.when(r != 0)(upper)
    recv_z(1, 0)
    section(1, 1, 1)
    recv_z(1, 1)
    recv_z(1, 2)
    section(1, 2, 3)
    recv_x(1, 0)
    section(1, 0, 1)
    recv_x(1, 1)
    section(1, 15, 1)
    recv_z(1, 3)
    recv_z(1, 4)
    section(1, 5, 5)

    pl.when(r == 0)(lambda: each_slot(forwarded))
    for stage in range(2):
        for n in range(NG):
            sent_z(stage, n)
        for side in range(2):
            sent_x(stage, side)


def store(src, dst, sem):
    copies = []
    for c in range(3):
        for i in range(4):
            part = pl.ds(4 * i, 4)
            copies.append(pltpu.make_async_copy(src.at[c, part], dst.at[c, part], sem.at[c, i]))
    for copy in copies:
        copy.start()
    for copy in copies:
        copy.wait()


def local(velocity, noise, previous, decay, stress_factor, mean_profile):
    vmem = pl.BlockSpec(memory_space=pltpu.VMEM)
    hbm = pl.BlockSpec(memory_space=pl.ANY)
    dma = pltpu.SemaphoreType.DMA
    buffers = [
        (3, NX + 2, NZ, NY), (3, NX + 2, NZ, NY), (2, 2, 3, NX, 1, NY),
        (SLOTS, 3, DEPTH, SPAN), (3, DEPTH, SPAN), (SLOTS, 2, DEPTH, 128), (SLOTS, 2, DEPTH, 128),
        (SLOTS, 3, 2, 4, 2, NZ, SPAN), (SLOTS, 2, 4, 3, 2, NZ, SPAN),
        (PL, 2, 2, 4, 3, NZ, SPAN), (3, NZ, NY), (10, NZ, 128), (3, DEPTH, 128),
    ]
    call = pl.pallas_call(
        kernel,
        out_shape=pltpu.VMEM((3, NX, NZ, NY), F32),
        in_specs=[hbm, hbm, hbm] + [vmem] * 6,
        out_specs=vmem,
        scratch_shapes=[pltpu.VMEM(shape, F32) for shape in buffers]
        + [
            dma((SLOTS + 3,)), dma((SLOTS, 2)), dma((SLOTS, 2)), dma((SLOTS, 4, 2)), dma((SLOTS, 4, 2)),
            dma((SLOTS, 2, 2)), dma((PL, 2, 2)), dma((SLOTS,)),
            dma((2, 2, NG)), dma((2, 2, NG)), dma((2, 2)), dma((2, 2)),
        ],
        compiler_params=pltpu.CompilerParams(
            collective_id=0, has_side_effects=True, vmem_limit_bytes=48 * 2**20
        ),
        name="inflow_step",
    )
    done = call(
        velocity, noise, previous, decay, stress_factor, mean_profile[None, :],
        *(jnp.asarray(w) for w in weights()),
    )
    return pl.pallas_call(
        store,
        out_shape=jax.ShapeDtypeStruct(done.shape, F32),
        in_specs=[vmem],
        out_specs=hbm,
        scratch_shapes=[dma((3, 4))],
        compiler_params=pltpu.CompilerParams(vmem_limit_bytes=2**20),
        name="store",
    )(done)


def solution(mesh):
    placed = (
        P(None, "grp", "gx", None),
        P(None, None, None, "gx"),
        P(None, None, "gx"),
        P(),
        P(),
        P(),
    )
    return jax.shard_map(
        local, mesh=mesh, in_specs=placed, out_specs=P(None, "grp", "gx", None), check_vma=False
    )
```
